32 devices in a mesh: ia: 4 (over x, core), ja: 4 (over z), ka: 2 (over y).
Axes of the slice: x: 2, y: 2, z: 4, core: 2. Of those that a mesh axis runs over, the one named last changes fastest.
Arguments:
- tensor: bfloat16 [768, 256, 256], P('ia', 'ja', 'ka'), may hold values from -190 to 190
- matrix: bfloat16 [768, 4096], P('ia', ('ja', 'ka')), may hold values from -160 to 160
- second_in: float32 [256, 256], P('ja'), may hold values from -10 to 10
- third_in: float32 [256, 256], P('ka'), may hold values from -10 to 10
- column_in: float32 [4096, 256], P(('ja', 'ka')), may hold values from -510 to 510
Outputs:
- first_out: float32 [768, 256], P(('ia', 'ja', 'ka'))
- second_out: float32 [4, 64, 256], P('ja', ('ia', 'ka'))
- third_out: float32 [2, 128, 256], P('ka', ('ia', 'ja'))
- column_out: float32 [8, 512, 256], P(('ja', 'ka'), 'ia')
The draws below stay inside these ranges and needn't reach their ends.
All inputs are finite; a program needn't handle non-finite values.
Results may differ from the reference program's by a relative error of at most 0.02.
Values may be sent and summed in bfloat16 or wider, within the bound.
A program may use at most 64 MiB of HBM per device.

```python
import math
import jax
import jax.numpy as jnp
from jax import lax

R = 256
JB = 64
KB = 128
MB = 512
I = 768
J = 256
K = 256
M = 4096


def ramp(length, end_ratio):
    position = jnp.arange(length, dtype=jnp.float32) / max(length - 1, 1)
    return jnp.exp(math.log(end_ratio) * (position - 0.5))


def draw_tensor(key, part):
    subkeys = jax.random.split(jax.random.fold_in(key, 11), 1)
    noise_cells = jnp.clip(jax.random.normal(subkeys[0], (I, J, K), jnp.float32), -4.0, 4.0)
    profile = ramp(I, math.sqrt(10.0))[:, None, None] * ramp(J, math.sqrt(10.0))[None, :, None] * ramp(K, math.sqrt(10.0))[None, None, :]
    values = profile * noise_cells
    return values.astype(jnp.bfloat16)


def draw_matrix(key, part):
    subkeys = jax.random.split(jax.random.fold_in(key, 23), 1)
    noise_cells = jnp.clip(jax.random.normal(subkeys[0], (I, M), jnp.float32), -4.0, 4.0)
    profile = ramp(I, math.sqrt(10.0))[:, None] * ramp(M, math.sqrt(10.0))[None, :]
    values = 3.0 * profile * noise_cells
    return values.astype(jnp.bfloat16)


def factor_draw(key, length):
    subkeys = jax.random.split(key, 3)
    row_common = jnp.clip(jax.random.normal(subkeys[1], (length,), jnp.float32), -3.0, 3.0)
    column_weight = 1.0 + 0.5 * jnp.clip(jax.random.normal(subkeys[2], (R,), jnp.float32), -3.0, 3.0)
    noise_cells = jnp.clip(jax.random.normal(subkeys[0], (length, R), jnp.float32), -4.0, 4.0)
    return noise_cells + 0.7 * row_common[:, None] * column_weight[None, :]


def draw_second_in(key, part):
    return factor_draw(jax.random.fold_in(key, 31), J)


def draw_third_in(key, part):
    return factor_draw(jax.random.fold_in(key, 37), K)


def draw_column_in(key, part):
    base = factor_draw(jax.random.fold_in(key, 41), M)
    weight_scale = math.sqrt(J * K / M)
    profile = ramp(M, 4.0)
    return base * profile[:, None] * weight_scale


def setup_inputs(seed: int = 0) -> dict:
    streams_of = jax.random.split(jax.random.key(seed), 6)
    return {
        "tensor": draw_tensor(jax.random.fold_in(streams_of[5], 71), 0),
        "matrix": draw_matrix(jax.random.fold_in(streams_of[5], 71), 0),
        "second_in": draw_second_in(jax.random.fold_in(streams_of[5], 71), 0),
        "third_in": draw_third_in(jax.random.fold_in(streams_of[5], 71), 0),
        "column_in": draw_column_in(jax.random.fold_in(streams_of[5], 71), 0),
    }


def gram_of(factor):
    return jnp.dot(factor.T.astype(jnp.float32), factor.astype(jnp.float32), precision=lax.Precision.HIGHEST, preferred_element_type=jnp.float32)

def solve_rows(right_side, system):
    lower_factor = jnp.linalg.cholesky(system)
    return jax.scipy.linalg.cho_solve((lower_factor, True), right_side.T).T

def normalize(unscaled):
    return unscaled * lax.rsqrt(lax.optimization_barrier(jnp.mean(unscaled * unscaled, axis=0)) + 1e-06)

def reference(tensor, matrix, second_in, third_in, column_in):
    gram_second = gram_of(second_in)
    gram_third = gram_of(third_in)
    gram_column = gram_of(column_in)
    column_half = column_in.astype(jnp.bfloat16)
    weights_one = (second_in[:, None, :] * third_in[None, :, :]).astype(jnp.bfloat16)
    partial_one = lax.dot_general(tensor.astype(jnp.float32), weights_one.astype(jnp.float32), (((1, 2), (0, 1)), ((), ())), preferred_element_type=jnp.float32)
    partial_one = partial_one + jnp.dot(matrix.astype(jnp.float32), column_half.astype(jnp.float32), preferred_element_type=jnp.float32)
    first_new = normalize(solve_rows(partial_one, gram_second * gram_third + gram_column))
    gram_first = gram_of(first_new)
    first_half = first_new.astype(jnp.bfloat16)
    weights_two = (first_half.astype(jnp.float32)[:, None, :] * third_in[None, :, :]).astype(jnp.bfloat16)
    partial_two = lax.dot_general(tensor.astype(jnp.float32), weights_two.astype(jnp.float32), (((0, 2), (0, 1)), ((), ())), preferred_element_type=jnp.float32)
    second_new = normalize(solve_rows(partial_two, gram_first * gram_third))
    gram_updated = gram_of(second_new)
    second_half = second_new.astype(jnp.bfloat16)
    tensor_blocks = tensor.reshape(I // 32, 32, J, K)
    half_blocks = first_half.reshape(I // 32, 32, R)

    def add_block(running, slab_pair):
        tensor_slab, half_slab = slab_pair
        weights_three = half_slab[:, None, :] * second_half[None, :, :]
        term = lax.dot_general(tensor_slab.astype(jnp.float32), weights_three.astype(jnp.float32), (((0, 1), (0, 1)), ((), ())), preferred_element_type=jnp.float32)
        return (running + term, None)
    partial_three, unused = lax.scan(add_block, jnp.zeros((K, R), jnp.float32), (tensor_blocks, half_blocks))
    third_new = normalize(solve_rows(partial_three, gram_first * gram_updated))
    partial_column = lax.dot_general(matrix.astype(jnp.float32), first_half.astype(jnp.float32), (((0,), (0,)), ((), ())), preferred_element_type=jnp.float32)
    column_new = normalize(solve_rows(partial_column, gram_first))
    return (first_new, second_new.reshape(J // JB, JB, R), third_new.reshape(K // KB, KB, R), column_new.reshape(M // MB, MB, R))
```

```python
import functools

import jax
import jax.numpy as jnp
from jax import lax
from jax.experimental import pallas as pl
from jax.experimental.pallas import tpu as pltpu
from jax.sharding import PartitionSpec as P

AXES = ("ia", "ja", "ka")
MESH = pl.DeviceIdType.MESH
HIGH = lax.Precision.HIGHEST
VMEM_LIMIT = 48 * 1024 * 1024


def dot_high(left, right, dims=(((1,), (0,)), ((), ()))):
    return lax.dot_general(
        left, right, dims, precision=HIGH, preferred_element_type=jnp.float32
    )


def gram_of(factor):
    return dot_high(factor, factor, (((0,), (0,)), ((), ())))


def group_size(sizes, axes):
    total = 1
    for axis in axes:
        total *= sizes[axis]
    return total


def place_in(sizes, axes):
    place = 0
    for axis in axes:
        place = place * sizes[axis] + lax.axis_index(axis)
    return place


def device_at(sizes, axes, place):
    coords = {}
    for axis in reversed(axes):
        coords[axis] = lax.rem(place, sizes[axis])
        place = place // sizes[axis]
    return tuple(coords[a] if a in coords else lax.axis_index(a) for a in AXES)


def enter(sizes, axes):
    count = group_size(sizes, axes)
    me = place_in(sizes, axes)
    barrier = pltpu.get_barrier_semaphore()

    def greet(step, carry):
        peer = lax.rem(me + step, count)
        pl.semaphore_signal(
            barrier, inc=1, device_id=device_at(sizes, axes, peer), device_id_type=MESH
        )
        return carry

    lax.fori_loop(1, count, greet, 0)
    pl.semaphore_wait(barrier, count - 1)


class Exchange:
    def __init__(self, sizes, axes, source, target, sems):
        self.sizes, self.axes = sizes, axes
        self.count = group_size(sizes, axes)
        self.me = place_in(sizes, axes)
        self.source, self.target, self.sems = source, target, sems

    def copy(self, step):
        peer = lax.rem(self.me + step, self.count)
        return pltpu.make_async_remote_copy(
            src_ref=self.source(peer),
            dst_ref=self.target(step, self.me),
            send_sem=self.sems.at[0, step],
            recv_sem=self.sems.at[1, step],
            device_id=device_at(self.sizes, self.axes, peer),
            device_id_type=MESH,
        )

    def start(self):
        def one(step, carry):
            self.copy(step).start()
            return carry

        lax.fori_loop(1, self.count, one, 0)

    def wait(self):
        def one(step, carry):
            self.copy(step).wait()
            return carry

        lax.fori_loop(1, self.count, one, 0)


def add_slots(first, slots, count):
    return lax.fori_loop(1, count, lambda step, total: total + slots[step], first)


def inverse_kernel(block, a_ref, out_ref):
    many, width, _ = a_ref.shape
    out_ref[...] = a_ref[...]
    lane = lax.broadcasted_iota(jnp.int32, (block, block), 1)
    line = lax.broadcasted_iota(jnp.int32, (block, block), 0)
    wide_lane = lax.broadcasted_iota(jnp.int32, (block, width), 1)
    wide_line = lax.broadcasted_iota(jnp.int32, (block, width), 0)
    for start in range(0, width, block):
        stop = start + block
        rows = [out_ref[m, start:stop, :] for m in range(many)]
        pivots = [r[:, start:stop] for r in rows]
        for k in range(block):
            cross = (lane == k) | (line == k)
            for m in range(many):
                d = pivots[m]
                scale = 1.0 / d[k : k + 1, k : k + 1]
                row = jnp.where(lane[:1] == k, -1.0, d[k : k + 1, :]) * scale
                col = jnp.where(line[:, :1] == k, -1.0, d[:, k : k + 1])
                pivots[m] = jnp.where(cross, 0.0, d) - col * row
        own = (wide_lane >= start) & (wide_lane < stop)
        picked = jnp.where(wide_lane == wide_line + start, -1.0, 0.0)
        for m in range(many):
            sides = jnp.where(own, picked, rows[m])
            scaled = dot_high(pivots[m], sides)
            update = dot_high(sides, scaled, (((0,), (0,)), ((), ())))
            whole = out_ref[m]
            at_line = lax.broadcasted_iota(jnp.int32, whole.shape, 0)
            at_lane = lax.broadcasted_iota(jnp.int32, whole.shape, 1)
            gone = ((at_line >= start) & (at_line < stop)) | (
                (at_lane >= start) & (at_lane < stop)
            )
            out_ref[m] = jnp.where(gone, 0.0, whole) + update
    out_ref[...] = -out_ref[...]


def inverses(*systems):
    stacked = jnp.stack(systems)
    block = 64 if stacked.shape[-1] % 64 == 0 else 8
    out = pl.pallas_call(
        functools.partial(inverse_kernel, block),
        out_shape=jax.ShapeDtypeStruct(stacked.shape, jnp.float32),
        in_specs=[pl.BlockSpec(memory_space=pltpu.VMEM)],
        out_specs=pl.BlockSpec(memory_space=pltpu.VMEM),
        compiler_params=pltpu.CompilerParams(vmem_limit_bytes=VMEM_LIMIT),
    )(stacked)
    return [out[m] for m in range(len(systems))]


def call(kernel, outs, scratch, ident, *operands):
    return pl.pallas_call(
        kernel,
        out_shape=outs,
        in_specs=[pl.BlockSpec(memory_space=pltpu.VMEM)] * len(operands),
        out_specs=[pl.BlockSpec(memory_space=pltpu.VMEM)] * len(outs),
        scratch_shapes=scratch,
        compiler_params=pltpu.CompilerParams(
            collective_id=ident, has_side_effects=True, vmem_limit_bytes=VMEM_LIMIT
        ),
    )(*operands)


def sems(count):
    return pltpu.SemaphoreType.DMA((2, count))


def shape(*dims, dtype=jnp.float32):
    return jax.ShapeDtypeStruct(dims, dtype)


def system_kernel(sizes, grams, third, system, gram_third, got, thirds, stage, s0, s1, s2):
    group = ("ja", "ka")
    count, rows = grams.shape[0], grams.shape[1] // 2
    enter(sizes, group)
    spread = Exchange(sizes, group, lambda p: grams.at[p], lambda s, me: got.at[s], s0)
    share = Exchange(sizes, ("ka",), lambda p: third, lambda s, me: thirds.at[s], s1)
    spread.start()
    share.start()
    total = gram_of(third[...])
    share.wait()
    for step in range(1, sizes["ka"]):
        total = total + gram_of(thirds[step])
    gram_third[...] = total
    spread.wait()
    me = spread.me
    summed = add_slots(grams[me], got, count)
    mine = summed[:rows] * gram_third[pl.ds(pl.multiple_of(me * rows, 8), rows), :]
    mine = mine + summed[rows:]
    stage[...] = mine
    system[me] = mine
    spread_back = Exchange(sizes, group, lambda p: stage, lambda s, me: system.at[me], s2)
    spread_back.start()
    spread_back.wait()


def solve_kernel(sizes, group, with_column, *refs):
    if with_column:
        pieces, inverse, column, mine, wide, column_sum, got, got_column, stage, s0, s1, s2 = refs
    else:
        pieces, inverse, mine, wide, got, stage, s0, s1 = refs
    enter(sizes, AXES)
    spread = Exchange(sizes, group, lambda p: pieces.at[p], lambda s, me: got.at[s], s0)
    spread.start()
    if with_column:
        side = Exchange(
            sizes, ("ia",), lambda p: column.at[p], lambda s, me: got_column.at[s], s2
        )
        side.start()
    spread.wait()
    raw = dot_high(add_slots(pieces[spread.me], got, spread.count), inverse[...])
    mine[...] = raw
    stage[...] = raw
    back = Exchange(sizes, AXES, lambda p: stage, lambda s, me: wide.at[me], s1)
    wide[back.me] = raw
    back.start()
    if with_column:
        side.wait()
        total = column[side.me].astype(jnp.float32)
        for step in range(1, sizes["ia"]):
            total = total + got_column[step].astype(jnp.float32)
        column_sum[...] = total
    back.wait()


def solve_shared(sizes, group, ident, pieces, inverse, column=None):
    count, rows, width = pieces.shape
    everyone = group_size(sizes, AXES)
    outs = [shape(rows, width), shape(everyone, rows, width)]
    scratch = [pltpu.VMEM(pieces.shape, jnp.float32)]
    operands = [pieces, inverse]
    tail = [sems(count), sems(everyone)]
    if column is not None:
        outs.append(shape(*column.shape[1:]))
        scratch.append(pltpu.VMEM(column.shape, column.dtype))
        operands.append(column)
        tail.append(sems(column.shape[0]))
    scratch.append(pltpu.VMEM((rows, width), jnp.float32))
    kernel = functools.partial(solve_kernel, sizes, group, column is not None)
    return call(kernel, outs, scratch + tail, ident, *operands)


def last_kernel(
    sizes, totals, pieces, inverse, column, third, column_out, got, stage, sums, s0, s1
):
    group = ("ia", "ja")
    enter(sizes, AXES)
    spread = Exchange(sizes, group, lambda p: pieces.at[p], lambda s, me: got.at[s], s0)
    spread.start()
    column_raw = column[...]
    column_square = jnp.sum(column_raw * column_raw, axis=0, keepdims=True)
    spread.wait()
    raw = dot_high(add_slots(pieces[spread.me], got, spread.count), inverse[...])
    square = jnp.sum(raw * raw, axis=0, keepdims=True)
    line = lax.broadcasted_iota(jnp.int32, stage.shape, 0)
    mine = jnp.where(line == 0, square, jnp.where(line == 1, column_square, 0.0))
    stage[...] = mine
    back = Exchange(sizes, AXES, lambda p: stage, lambda s, me: sums.at[s], s1)
    back.start()
    back.wait()
    whole = add_slots(mine, sums, back.count)
    third[...] = raw * lax.rsqrt(whole[0:1] / totals[0] + 1e-06)
    column_out[...] = column_raw * lax.rsqrt(whole[1:2] / totals[1] + 1e-06)


def pieces_of(whole, count):
    rows = whole.shape[0] // count
    pieces = whole.reshape(count, rows, whole.shape[1])
    return jnp.pad(pieces, ((0, 0), (0, -rows % 8), (0, 0))), rows


def body(sizes, tensor, matrix, second_in, third_in, column_in):
    n_a, n_b, n_c = (sizes[a] for a in AXES)
    span_first, span_second, span_third = tensor.shape
    width = second_in.shape[1]
    total_first, total_second = span_first * n_a, span_second * n_b
    total_third, total_column = span_third * n_c, matrix.shape[1] * n_b * n_c
    everyone = n_a * n_b * n_c

    pair = n_b * n_c
    grams = jnp.concatenate(
        [
            (gram_of(second_in) * (1.0 / n_c)).reshape(pair, width // pair, width),
            gram_of(column_in).reshape(pair, width // pair, width),
        ],
        axis=1,
    )
    rows = width // pair
    system, gram_third = call(
        functools.partial(system_kernel, sizes),
        [shape(pair, rows, width), shape(width, width)],
        [
            pltpu.VMEM(grams.shape, jnp.float32),
            pltpu.VMEM((n_c,) + third_in.shape, jnp.float32),
            pltpu.VMEM((rows, width), jnp.float32),
            sems(pair),
            sems(n_c),
            sems(pair),
        ],
        0,
        grams,
        third_in,
    )
    (inverse_one,) = inverses(system.reshape(width, width))

    weights_one = (second_in[:, None, :] * third_in[None, :, :]).astype(jnp.bfloat16)
    first_whole = lax.dot_general(
        tensor, weights_one, (((1, 2), (0, 1)), ((), ())), preferred_element_type=jnp.float32
    )
    first_whole = first_whole + jnp.dot(
        matrix, column_in.astype(jnp.bfloat16), preferred_element_type=jnp.float32
    )
    pieces, rows_first = pieces_of(first_whole, pair)
    raw_one, wide = solve_shared(sizes, ("ja", "ka"), 1, pieces, inverse_one)
    first_all = wide[:, :rows_first].reshape(total_first, width)
    first_gram = gram_of(first_all)
    scaling = lax.rsqrt(jnp.sum(first_all * first_all, axis=0) / total_first + 1e-06)
    gram_first = first_gram * scaling[:, None] * scaling[None, :]
    first_new = raw_one[:rows_first] * scaling
    first_mine = lax.dynamic_slice_in_dim(
        first_all, lax.axis_index("ia") * span_first, span_first, 0
    )
    first_half = (first_mine * scaling).astype(jnp.bfloat16)

    weights_two = (first_half.astype(jnp.float32)[:, None, :] * third_in[None, :, :]).astype(
        jnp.bfloat16
    )
    second_whole = lax.dot_general(
        tensor, weights_two, (((0, 2), (0, 1)), ((), ())), preferred_element_type=jnp.float32
    )
    column_whole = lax.dot_general(
        matrix, first_half, (((0,), (0,)), ((), ())), preferred_element_type=jnp.float32
    )
    inverse_two, inverse_first = inverses(gram_first * gram_third, gram_first)
    pieces, rows_second = pieces_of(second_whole, n_a * n_c)
    column_pieces, rows_column = pieces_of(column_whole, n_a)
    raw_two, wide, column_sum = solve_shared(
        sizes, ("ia", "ka"), 2, pieces, inverse_two, column_pieces
    )
    second_all = wide[:, :rows_second].reshape(n_a, n_b, n_c, rows_second, width)
    second_all = second_all.transpose(1, 0, 2, 3, 4)
    second_mine = lax.dynamic_index_in_dim(second_all, lax.axis_index("ja"), 0, False)
    second_all = second_all.reshape(total_second, width)
    scaling = lax.rsqrt(jnp.sum(second_all * second_all, axis=0) / total_second + 1e-06)
    gram_updated = gram_of(second_all) * scaling[:, None] * scaling[None, :]
    second_new = raw_two[:rows_second] * scaling
    second_half = (second_mine.reshape(span_second, width) * scaling).astype(jnp.bfloat16)

    (inverse_three,) = inverses(gram_first * gram_updated)
    column_raw = dot_high(column_sum, inverse_first)
    weights_three = (first_half[:, None, :] * second_half[None, :, :]).reshape(
        span_first * span_second, width
    )
    third_whole = lax.dot_general(
        tensor.reshape(span_first * span_second, span_third),
        weights_three,
        (((0,), (0,)), ((), ())),
        preferred_element_type=jnp.float32,
    )
    pieces, rows_third = pieces_of(third_whole, n_a * n_b)
    third_new, column_new = call(
        functools.partial(last_kernel, sizes, (total_third, total_column)),
        [shape(*pieces.shape[1:]), shape(*column_raw.shape)],
        [
            pltpu.VMEM(pieces.shape, jnp.float32),
            pltpu.VMEM((8, width), jnp.float32),
            pltpu.VMEM((everyone, 8, width), jnp.float32),
            sems(pieces.shape[0]),
            sems(everyone),
        ],
        3,
        pieces,
        inverse_three,
        column_raw,
    )
    return (first_new, second_new[None], third_new[:rows_third][None], column_new[:rows_column][None])


def solution(mesh):
    placed = (
        P("ia", "ja", "ka"),
        P("ia", ("ja", "ka")),
        P("ja", None),
        P("ka", None),
        P(("ja", "ka"), None),
    )
    return jax.shard_map(
        functools.partial(body, dict(mesh.shape)),
        mesh=mesh,
        in_specs=placed,
        out_specs=(
            P(("ia", "ja", "ka"), None),
            P("ja", ("ia", "ka"), None),
            P("ka", ("ia", "ja"), None),
            P(("ja", "ka"), "ia", None),
        ),
        check_vma=False,
    )
```

```python
import functools

import jax
import jax.numpy as jnp
from jax import lax
from jax.experimental import pallas as pl
from jax.experimental.pallas import tpu as pltpu
from jax.sharding import PartitionSpec as P

AXES = ("ia", "ja", "ka")
MESH = pl.DeviceIdType.MESH
HIGH = lax.Precision.HIGHEST
VMEM_LIMIT = 48 * 1024 * 1024


def dot_high(left, right, dims=(((1,), (0,)), ((), ()))):
    return lax.dot_general(
        left, right, dims, precision=HIGH, preferred_element_type=jnp.float32
    )


def gram_of(factor):
    return dot_high(factor, factor, (((0,), (0,)), ((), ())))


def group_size(sizes, axes):
    total = 1
    for axis in axes:
        total *= sizes[axis]
    return total


def place_in(sizes, axes):
    place = 0
    for axis in axes:
        place = place * sizes[axis] + lax.axis_index(axis)
    return place


def device_at(sizes, axes, place):
    coords = {}
    for axis in reversed(axes):
        coords[axis] = lax.rem(place, sizes[axis])
        place = place // sizes[axis]
    return tuple(coords[a] if a in coords else lax.axis_index(a) for a in AXES)


def enter(sizes, axes):
    count = group_size(sizes, axes)
    me = place_in(sizes, axes)
    barrier = pltpu.get_barrier_semaphore()

    def greet(step, carry):
        peer = lax.rem(me + step, count)
        pl.semaphore_signal(
            barrier, inc=1, device_id=device_at(sizes, axes, peer), device_id_type=MESH
        )
        return carry

    lax.fori_loop(1, count, greet, 0)
    pl.semaphore_wait(barrier, count - 1)


class Exchange:
    def __init__(self, sizes, axes, source, target, sems):
        self.sizes, self.axes = sizes, axes
        self.count = group_size(sizes, axes)
        self.me = place_in(sizes, axes)
        self.source, self.target, self.sems = source, target, sems

    def copy(self, step):
        peer = lax.rem(self.me + step, self.count)
        return pltpu.make_async_remote_copy(
            src_ref=self.source(peer),
            dst_ref=self.target(step, self.me),
            send_sem=self.sems.at[0, step],
            recv_sem=self.sems.at[1, step],
            device_id=device_at(self.sizes, self.axes, peer),
            device_id_type=MESH,
        )

    def start(self):
        def one(step, carry):
            self.copy(step).start()
            return carry

        lax.fori_loop(1, self.count, one, 0)

    def wait(self):
        def one(step, carry):
            self.copy(step).wait()
            return carry

        lax.fori_loop(1, self.count, one, 0)


def add_slots(first, slots, count):
    return lax.fori_loop(1, count, lambda step, total: total + slots[step], first)


def sweep(d, k, few, lane, line, cross):
    top = lane[:1]
    small, below, scale, rows, cols = {}, {}, [], [], []
    for i in range(few):
        at = k + i
        rows.append(
            jnp.where((top >= k) & (top < k + few), jnp.where(top == at, -1.0, 0.0), d[at : at + 1, :])
        )
        side = line[:, :1]
        cols.append(
            jnp.where(
                (side >= k) & (side < k + few), jnp.where(side == at, -1.0, 0.0), d[:, at : at + 1]
            )
        )
        for j in range(i, few):
            small[i, j] = jnp.broadcast_to(d[at : at + 1, k + j : k + j + 1], top.shape)
    for p in range(few):
        scale.append(1.0 / small[p, p])
        for i in range(p + 1, few):
            below[i, p] = small[p, i] * scale[p]
            for j in range(i, few):
                small[i, j] = small[i, j] - below[i, p] * small[p, j]
    for i in range(few):
        for p in range(i):
            rows[i] = rows[i] - below[i, p] * rows[p]
    solved = [rows[i] * scale[i] for i in range(few)]
    for i in reversed(range(few)):
        for p in range(i + 1, few):
            solved[i] = solved[i] - below[p, i] * solved[p]
    total = jnp.where(cross, 0.0, d)
    for i in range(few):
        total = total - cols[i] * solved[i]
    return total


def inverse_kernel(block, few, a_ref, out_ref):
    many, width, _ = a_ref.shape
    out_ref[...] = a_ref[...]
    lane = lax.broadcasted_iota(jnp.int32, (block, block), 1)
    line = lax.broadcasted_iota(jnp.int32, (block, block), 0)
    wide_lane = lax.broadcasted_iota(jnp.int32, (block, width), 1)
    wide_line = lax.broadcasted_iota(jnp.int32, (block, width), 0)
    for start in range(0, width, block):
        stop = start + block
        rows = [out_ref[m, start:stop, :] for m in range(many)]
        pivots = [r[:, start:stop] for r in rows]
        for k in range(0, block, few):
            cross = ((lane >= k) & (lane < k + few)) | ((line >= k) & (line < k + few))
            for m in range(many):
                pivots[m] = sweep(pivots[m], k, few, lane, line, cross)
        own = (wide_lane >= start) & (wide_lane < stop)
        picked = jnp.where(wide_lane == wide_line + start, -1.0, 0.0)
        for m in range(many):
            sides = jnp.where(own, picked, rows[m])
            scaled = dot_high(pivots[m], sides)
            update = dot_high(sides, scaled, (((0,), (0,)), ((), ())))
            whole = out_ref[m]
            at_line = lax.broadcasted_iota(jnp.int32, whole.shape, 0)
            at_lane = lax.broadcasted_iota(jnp.int32, whole.shape, 1)
            gone = ((at_line >= start) & (at_line < stop)) | (
                (at_lane >= start) & (at_lane < stop)
            )
            out_ref[m] = jnp.where(gone, 0.0, whole) + update
    out_ref[...] = -out_ref[...]


def inverses(*systems):
    stacked = jnp.stack(systems)
    block = 64 if stacked.shape[-1] % 64 == 0 else 8
    out = pl.pallas_call(
        functools.partial(inverse_kernel, block, 4),
        out_shape=jax.ShapeDtypeStruct(stacked.shape, jnp.float32),
        in_specs=[pl.BlockSpec(memory_space=pltpu.VMEM)],
        out_specs=pl.BlockSpec(memory_space=pltpu.VMEM),
        compiler_params=pltpu.CompilerParams(vmem_limit_bytes=VMEM_LIMIT),
    )(stacked)
    return [out[m] for m in range(len(systems))]


def call(kernel, outs, scratch, ident, *operands):
    return pl.pallas_call(
        kernel,
        out_shape=outs,
        in_specs=[pl.BlockSpec(memory_space=pltpu.VMEM)] * len(operands),
        out_specs=[pl.BlockSpec(memory_space=pltpu.VMEM)] * len(outs),
        scratch_shapes=scratch,
        compiler_params=pltpu.CompilerParams(
            collective_id=ident, has_side_effects=True, vmem_limit_bytes=VMEM_LIMIT
        ),
    )(*operands)


def sems(count):
    return pltpu.SemaphoreType.DMA((2, count))


def shape(*dims, dtype=jnp.float32):
    return jax.ShapeDtypeStruct(dims, dtype)


def system_kernel(sizes, grams, third, system, gram_third, got, thirds, stage, s0, s1, s2):
    group = ("ja", "ka")
    count, rows = grams.shape[0], grams.shape[1] // 2
    enter(sizes, group)
    spread = Exchange(sizes, group, lambda p: grams.at[p], lambda s, me: got.at[s], s0)
    share = Exchange(sizes, ("ka",), lambda p: third, lambda s, me: thirds.at[s], s1)
    spread.start()
    share.start()
    total = gram_of(third[...])
    share.wait()
    for step in range(1, sizes["ka"]):
        total = total + gram_of(thirds[step])
    gram_third[...] = total
    spread.wait()
    me = spread.me
    summed = add_slots(grams[me], got, count)
    mine = summed[:rows] * gram_third[pl.ds(pl.multiple_of(me * rows, 8), rows), :]
    mine = mine + summed[rows:]
    stage[...] = mine
    system[me] = mine
    spread_back = Exchange(sizes, group, lambda p: stage, lambda s, me: system.at[me], s2)
    spread_back.start()
    spread_back.wait()


def solve_kernel(sizes, group, with_column, *refs):
    if with_column:
        pieces, inverse, column, mine, wide, column_sum, got, got_column, stage, s0, s1, s2 = refs
    else:
        pieces, inverse, mine, wide, got, stage, s0, s1 = refs
    enter(sizes, AXES)
    spread = Exchange(sizes, group, lambda p: pieces.at[p], lambda s, me: got.at[s], s0)
    spread.start()
    if with_column:
        side = Exchange(
            sizes, ("ia",), lambda p: column.at[p], lambda s, me: got_column.at[s], s2
        )
        side.start()
    spread.wait()
    raw = dot_high(add_slots(pieces[spread.me], got, spread.count), inverse[...])
    mine[...] = raw
    stage[...] = raw
    back = Exchange(sizes, AXES, lambda p: stage, lambda s, me: wide.at[me], s1)
    wide[back.me] = raw
    back.start()
    if with_column:
        side.wait()
        total = column[side.me].astype(jnp.float32)
        for step in range(1, sizes["ia"]):
            total = total + got_column[step].astype(jnp.float32)
        column_sum[...] = total
    back.wait()


def solve_shared(sizes, group, ident, pieces, inverse, column=None):
    count, rows, width = pieces.shape
    everyone = group_size(sizes, AXES)
    outs = [shape(rows, width), shape(everyone, rows, width)]
    scratch = [pltpu.VMEM(pieces.shape, jnp.float32)]
    operands = [pieces, inverse]
    tail = [sems(count), sems(everyone)]
    if column is not None:
        outs.append(shape(*column.shape[1:]))
        scratch.append(pltpu.VMEM(column.shape, column.dtype))
        operands.append(column)
        tail.append(sems(column.shape[0]))
    scratch.append(pltpu.VMEM((rows, width), jnp.float32))
    kernel = functools.partial(solve_kernel, sizes, group, column is not None)
    return call(kernel, outs, scratch + tail, ident, *operands)


def last_kernel(
    sizes, totals, pieces, inverse, column, third, column_out, got, stage, sums, s0, s1
):
    group = ("ia", "ja")
    enter(sizes, AXES)
    spread = Exchange(sizes, group, lambda p: pieces.at[p], lambda s, me: got.at[s], s0)
    spread.start()
    column_raw = column[...]
    column_square = jnp.sum(column_raw * column_raw, axis=0, keepdims=True)
    spread.wait()
    raw = dot_high(add_slots(pieces[spread.me], got, spread.count), inverse[...])
    square = jnp.sum(raw * raw, axis=0, keepdims=True)
    line = lax.broadcasted_iota(jnp.int32, stage.shape, 0)
    mine = jnp.where(line == 0, square, jnp.where(line == 1, column_square, 0.0))
    stage[...] = mine
    back = Exchange(sizes, AXES, lambda p: stage, lambda s, me: sums.at[s], s1)
    back.start()
    back.wait()
    whole = add_slots(mine, sums, back.count)
    third[...] = raw * lax.rsqrt(whole[0:1] / totals[0] + 1e-06)
    column_out[...] = column_raw * lax.rsqrt(whole[1:2] / totals[1] + 1e-06)


def pieces_of(whole, count):
    rows = whole.shape[0] // count
    pieces = whole.reshape(count, rows, whole.shape[1])
    return jnp.pad(pieces, ((0, 0), (0, -rows % 8), (0, 0))), rows


def body(sizes, tensor, matrix, second_in, third_in, column_in):
    n_a, n_b, n_c = (sizes[a] for a in AXES)
    span_first, span_second, span_third = tensor.shape
    width = second_in.shape[1]
    total_first, total_second = span_first * n_a, span_second * n_b
    total_third, total_column = span_third * n_c, matrix.shape[1] * n_b * n_c
    everyone = n_a * n_b * n_c

    pair = n_b * n_c
    grams = jnp.concatenate(
        [
            (gram_of(second_in) * (1.0 / n_c)).reshape(pair, width // pair, width),
            gram_of(column_in).reshape(pair, width // pair, width),
        ],
        axis=1,
    )
    rows = width // pair
    system, gram_third = call(
        functools.partial(system_kernel, sizes),
        [shape(pair, rows, width), shape(width, width)],
        [
            pltpu.VMEM(grams.shape, jnp.float32),
            pltpu.VMEM((n_c,) + third_in.shape, jnp.float32),
            pltpu.VMEM((rows, width), jnp.float32),
            sems(pair),
            sems(n_c),
            sems(pair),
        ],
        0,
        grams,
        third_in,
    )
    (inverse_one,) = inverses(system.reshape(width, width))

    weights_one = (second_in[:, None, :] * third_in[None, :, :]).astype(jnp.bfloat16)
    first_whole = lax.dot_general(
        tensor, weights_one, (((1, 2), (0, 1)), ((), ())), preferred_element_type=jnp.float32
    )
    first_whole = first_whole + jnp.dot(
        matrix, column_in.astype(jnp.bfloat16), preferred_element_type=jnp.float32
    )
    pieces, rows_first = pieces_of(first_whole, pair)
    raw_one, wide = solve_shared(sizes, ("ja", "ka"), 1, pieces, inverse_one)
    first_all = wide[:, :rows_first].reshape(total_first, width)
    first_gram = gram_of(first_all)
    scaling = lax.rsqrt(jnp.sum(first_all * first_all, axis=0) / total_first + 1e-06)
    gram_first = first_gram * scaling[:, None] * scaling[None, :]
    first_new = raw_one[:rows_first] * scaling
    first_mine = lax.dynamic_slice_in_dim(
        first_all, lax.axis_index("ia") * span_first, span_first, 0
    )
    first_half = (first_mine * scaling).astype(jnp.bfloat16)

    weights_two = (first_half.astype(jnp.float32)[:, None, :] * third_in[None, :, :]).astype(
        jnp.bfloat16
    )
    second_whole = lax.dot_general(
        tensor, weights_two, (((0, 2), (0, 1)), ((), ())), preferred_element_type=jnp.float32
    )
    column_whole = lax.dot_general(
        matrix, first_half, (((0,), (0,)), ((), ())), preferred_element_type=jnp.float32
    )
    inverse_two, inverse_first = inverses(gram_first * gram_third, gram_first)
    pieces, rows_second = pieces_of(second_whole, n_a * n_c)
    column_pieces, rows_column = pieces_of(column_whole, n_a)
    raw_two, wide, column_sum = solve_shared(
        sizes, ("ia", "ka"), 2, pieces, inverse_two, column_pieces
    )
    second_all = wide[:, :rows_second].reshape(n_a, n_b, n_c, rows_second, width)
    second_all = second_all.transpose(1, 0, 2, 3, 4)
    second_mine = lax.dynamic_index_in_dim(second_all, lax.axis_index("ja"), 0, False)
    second_all = second_all.reshape(total_second, width)
    scaling = lax.rsqrt(jnp.sum(second_all * second_all, axis=0) / total_second + 1e-06)
    gram_updated = gram_of(second_all) * scaling[:, None] * scaling[None, :]
    second_new = raw_two[:rows_second] * scaling
    second_half = (second_mine.reshape(span_second, width) * scaling).astype(jnp.bfloat16)

    (inverse_three,) = inverses(gram_first * gram_updated)
    column_raw = dot_high(column_sum, inverse_first)
    weights_three = (first_half[:, None, :] * second_half[None, :, :]).reshape(
        span_first * span_second, width
    )
    third_whole = lax.dot_general(
        tensor.reshape(span_first * span_second, span_third),
        weights_three,
        (((0,), (0,)), ((), ())),
        preferred_element_type=jnp.float32,
    )
    pieces, rows_third = pieces_of(third_whole, n_a * n_b)
    third_new, column_new = call(
        functools.partial(last_kernel, sizes, (total_third, total_column)),
        [shape(*pieces.shape[1:]), shape(*column_raw.shape)],
        [
            pltpu.VMEM(pieces.shape, jnp.float32),
            pltpu.VMEM((8, width), jnp.float32),
            pltpu.VMEM((everyone, 8, width), jnp.float32),
            sems(pieces.shape[0]),
            sems(everyone),
        ],
        3,
        pieces,
        inverse_three,
        column_raw,
    )
    return (first_new, second_new[None], third_new[:rows_third][None], column_new[:rows_column][None])


def solution(mesh):
    placed = (
        P("ia", "ja", "ka"),
        P("ia", ("ja", "ka")),
        P("ja", None),
        P("ka", None),
        P(("ja", "ka"), None),
    )
    return jax.shard_map(
        functools.partial(body, dict(mesh.shape)),
        mesh=mesh,
        in_specs=placed,
        out_specs=(
            P(("ia", "ja", "ka"), None),
            P("ja", ("ia", "ka"), None),
            P("ka", ("ia", "ja"), None),
            P(("ja", "ka"), "ia", None),
        ),
        check_vma=False,
    )
```

```python
import functools

import jax
import jax.numpy as jnp
from jax import lax
from jax.experimental import pallas as pl
from jax.experimental.pallas import tpu as pltpu
from jax.sharding import PartitionSpec as P

AXES = ("ia", "ja", "ka")
MESH = pl.DeviceIdType.MESH
HIGH = lax.Precision.HIGHEST
VMEM_LIMIT = 48 * 1024 * 1024


def dot_high(left, right, dims=(((1,), (0,)), ((), ()))):
    return lax.dot_general(
        left, right, dims, precision=HIGH, preferred_element_type=jnp.float32
    )


def gram_of(factor):
    return dot_high(factor, factor, (((0,), (0,)), ((), ())))


def group_size(sizes, axes):
    total = 1
    for axis in axes:
        total *= sizes[axis]
    return total


def place_in(sizes, axes):
    place = 0
    for axis in axes:
        place = place * sizes[axis] + lax.axis_index(axis)
    return place


def device_at(sizes, axes, place):
    coords = {}
    for axis in reversed(axes):
        coords[axis] = lax.rem(place, sizes[axis])
        place = place // sizes[axis]
    return tuple(coords[a] if a in coords else lax.axis_index(a) for a in AXES)


def enter(sizes, axes):
    count = group_size(sizes, axes)
    me = place_in(sizes, axes)
    barrier = pltpu.get_barrier_semaphore()

    def greet(step, carry):
        peer = lax.rem(me + step, count)
        pl.semaphore_signal(
            barrier, inc=1, device_id=device_at(sizes, axes, peer), device_id_type=MESH
        )
        return carry

    lax.fori_loop(1, count, greet, 0)
    pl.semaphore_wait(barrier, count - 1)


class Exchange:
    def __init__(self, sizes, axes, source, target, sems):
        self.sizes, self.axes = sizes, axes
        self.count = group_size(sizes, axes)
        self.me = place_in(sizes, axes)
        self.source, self.target, self.sems = source, target, sems

    def copy(self, step):
        peer = lax.rem(self.me + step, self.count)
        return pltpu.make_async_remote_copy(
            src_ref=self.source(peer),
            dst_ref=self.target(step, self.me),
            send_sem=self.sems.at[0, step],
            recv_sem=self.sems.at[1, step],
            device_id=device_at(self.sizes, self.axes, peer),
            device_id_type=MESH,
        )

    def start(self):
        def one(step, carry):
            self.copy(step).start()
            return carry

        lax.fori_loop(1, self.count, one, 0)

    def wait(self):
        def one(step, carry):
            self.copy(step).wait()
            return carry

        lax.fori_loop(1, self.count, one, 0)


def add_slots(first, slots, count):
    return lax.fori_loop(1, count, lambda step, total: total + slots[step], first)


def sweep(d, k, few, lane, line, cross):
    top = lane[:1]
    small, below, scale, rows, cols = {}, {}, [], [], []
    for i in range(few):
        at = k + i
        rows.append(
            jnp.where((top >= k) & (top < k + few), jnp.where(top == at, -1.0, 0.0), d[at : at + 1, :])
        )
        side = line[:, :1]
        cols.append(
            jnp.where(
                (side >= k) & (side < k + few), jnp.where(side == at, -1.0, 0.0), d[:, at : at + 1]
            )
        )
        for j in range(i, few):
            small[i, j] = jnp.broadcast_to(d[at : at + 1, k + j : k + j + 1], top.shape)
    for p in range(few):
        scale.append(1.0 / small[p, p])
        for i in range(p + 1, few):
            below[i, p] = small[p, i] * scale[p]
            for j in range(i, few):
                small[i, j] = small[i, j] - below[i, p] * small[p, j]
    for i in range(few):
        for p in range(i):
            rows[i] = rows[i] - below[i, p] * rows[p]
    solved = [rows[i] * scale[i] for i in range(few)]
    for i in reversed(range(few)):
        for p in range(i + 1, few):
            solved[i] = solved[i] - below[p, i] * solved[p]
    total = jnp.where(cross, 0.0, d)
    for i in range(few):
        total = total - cols[i] * solved[i]
    return total


def invert(block, few, a_ref, out_ref):
    many, width, _ = a_ref.shape
    out_ref[...] = a_ref[...]
    lane = lax.broadcasted_iota(jnp.int32, (block, block), 1)
    line = lax.broadcasted_iota(jnp.int32, (block, block), 0)
    wide_lane = lax.broadcasted_iota(jnp.int32, (block, width), 1)
    wide_line = lax.broadcasted_iota(jnp.int32, (block, width), 0)
    for start in range(0, width, block):
        stop = start + block
        rows = [out_ref[m, start:stop, :] for m in range(many)]
        pivots = [r[:, start:stop] for r in rows]
        for k in range(0, block, few):
            cross = ((lane >= k) & (lane < k + few)) | ((line >= k) & (line < k + few))
            for m in range(many):
                pivots[m] = sweep(pivots[m], k, few, lane, line, cross)
        own = (wide_lane >= start) & (wide_lane < stop)
        picked = jnp.where(wide_lane == wide_line + start, -1.0, 0.0)
        for m in range(many):
            sides = jnp.where(own, picked, rows[m])
            scaled = dot_high(pivots[m], sides)
            update = dot_high(sides, scaled, (((0,), (0,)), ((), ())))
            whole = out_ref[m]
            at_line = lax.broadcasted_iota(jnp.int32, whole.shape, 0)
            at_lane = lax.broadcasted_iota(jnp.int32, whole.shape, 1)
            gone = ((at_line >= start) & (at_line < stop)) | (
                (at_lane >= start) & (at_lane < stop)
            )
            out_ref[m] = jnp.where(gone, 0.0, whole) + update
    out_ref[...] = -out_ref[...]


def block_of(width):
    return 64 if width % 64 == 0 else 8


def call(kernel, outs, scratch, ident, *operands):
    return pl.pallas_call(
        kernel,
        out_shape=outs,
        in_specs=[pl.BlockSpec(memory_space=pltpu.VMEM)] * len(operands),
        out_specs=[pl.BlockSpec(memory_space=pltpu.VMEM)] * len(outs),
        scratch_shapes=scratch,
        compiler_params=pltpu.CompilerParams(
            collective_id=ident, has_side_effects=True, vmem_limit_bytes=VMEM_LIMIT
        ),
    )(*operands)


def sems(count):
    return pltpu.SemaphoreType.DMA((2, count))


def shape(*dims, dtype=jnp.float32):
    return jax.ShapeDtypeStruct(dims, dtype)


def system_kernel(sizes, grams, third, system, gram_third, got, thirds, stage, s0, s1, s2):
    group = ("ja", "ka")
    count, rows = grams.shape[0], grams.shape[1] // 2
    enter(sizes, group)
    spread = Exchange(sizes, group, lambda p: grams.at[p], lambda s, me: got.at[s], s0)
    share = Exchange(sizes, ("ka",), lambda p: third, lambda s, me: thirds.at[s], s1)
    spread.start()
    share.start()
    total = gram_of(third[...])
    share.wait()
    for step in range(1, sizes["ka"]):
        total = total + gram_of(thirds[step])
    gram_third[...] = total
    spread.wait()
    me = spread.me
    summed = add_slots(grams[me], got, count)
    mine = summed[:rows] * gram_third[pl.ds(pl.multiple_of(me * rows, 8), rows), :]
    mine = mine + summed[rows:]
    stage[...] = mine
    system[me] = mine
    spread_back = Exchange(sizes, group, lambda p: stage, lambda s, me: system.at[me], s2)
    spread_back.start()
    spread_back.wait()


def solve_kernel(sizes, group, with_column, *refs):
    if with_column:
        pieces, systems, column, mine, wide, column_raw, got, inverse, stage, s0, s1 = refs[:11]
        got_column, s2 = refs[11:]
    else:
        pieces, systems, mine, wide, got, inverse, stage, s0, s1 = refs
    enter(sizes, AXES)
    spread = Exchange(sizes, group, lambda p: pieces.at[p], lambda s, me: got.at[s], s0)
    spread.start()
    if with_column:
        side = Exchange(
            sizes, ("ia",), lambda p: column.at[p], lambda s, me: got_column.at[s], s2
        )
        side.start()
    invert(block_of(systems.shape[-1]), 4, systems, inverse)
    spread.wait()
    raw = dot_high(add_slots(pieces[spread.me], got, spread.count), inverse[0])
    mine[...] = raw
    stage[...] = raw
    back = Exchange(sizes, AXES, lambda p: stage, lambda s, me: wide.at[me], s1)
    wide[back.me] = raw
    back.start()
    if with_column:
        side.wait()
        total = add_slots(column[side.me], got_column, side.count)
        column_raw[...] = dot_high(total, inverse[1])
    back.wait()


def solve_shared(sizes, group, ident, pieces, systems, column=None):
    count, rows, width = pieces.shape
    everyone = group_size(sizes, AXES)
    outs = [shape(rows, width), shape(everyone, rows, width)]
    scratch = [
        pltpu.VMEM(pieces.shape, jnp.float32),
        pltpu.VMEM(systems.shape, jnp.float32),
        pltpu.VMEM((rows, width), jnp.float32),
        sems(count),
        sems(everyone),
    ]
    operands = [pieces, systems]
    if column is not None:
        outs.append(shape(*column.shape[1:]))
        operands.append(column)
        scratch += [pltpu.VMEM(column.shape, column.dtype), sems(column.shape[0])]
    kernel = functools.partial(solve_kernel, sizes, group, column is not None)
    return call(kernel, outs, scratch, ident, *operands)


def last_kernel(
    sizes, totals, pieces, systems, column, third, column_out, got, inverse, stage, sums, s0, s1
):
    group = ("ia", "ja")
    enter(sizes, AXES)
    spread = Exchange(sizes, group, lambda p: pieces.at[p], lambda s, me: got.at[s], s0)
    spread.start()
    invert(block_of(systems.shape[-1]), 4, systems, inverse)
    column_raw = column[...]
    column_square = jnp.sum(column_raw * column_raw, axis=0, keepdims=True)
    spread.wait()
    raw = dot_high(add_slots(pieces[spread.me], got, spread.count), inverse[0])
    square = jnp.sum(raw * raw, axis=0, keepdims=True)
    line = lax.broadcasted_iota(jnp.int32, stage.shape, 0)
    mine = jnp.where(line == 0, square, jnp.where(line == 1, column_square, 0.0))
    stage[...] = mine
    back = Exchange(sizes, AXES, lambda p: stage, lambda s, me: sums.at[s], s1)
    back.start()
    back.wait()
    whole = add_slots(mine, sums, back.count)
    third[...] = raw * lax.rsqrt(whole[0:1] / totals[0] + 1e-06)
    column_out[...] = column_raw * lax.rsqrt(whole[1:2] / totals[1] + 1e-06)


def pieces_of(whole, count):
    rows = whole.shape[0] // count
    pieces = whole.reshape(count, rows, whole.shape[1])
    return jnp.pad(pieces, ((0, 0), (0, -rows % 8), (0, 0))), rows


def body(sizes, tensor, matrix, second_in, third_in, column_in):
    n_a, n_b, n_c = (sizes[a] for a in AXES)
    span_first, span_second, span_third = tensor.shape
    width = second_in.shape[1]
    total_first, total_second = span_first * n_a, span_second * n_b
    total_third, total_column = span_third * n_c, matrix.shape[1] * n_b * n_c
    everyone = n_a * n_b * n_c

    pair = n_b * n_c
    grams = jnp.concatenate(
        [
            (gram_of(second_in) * (1.0 / n_c)).reshape(pair, width // pair, width),
            gram_of(column_in).reshape(pair, width // pair, width),
        ],
        axis=1,
    )
    rows = width // pair
    system, gram_third = call(
        functools.partial(system_kernel, sizes),
        [shape(pair, rows, width), shape(width, width)],
        [
            pltpu.VMEM(grams.shape, jnp.float32),
            pltpu.VMEM((n_c,) + third_in.shape, jnp.float32),
            pltpu.VMEM((rows, width), jnp.float32),
            sems(pair),
            sems(n_c),
            sems(pair),
        ],
        0,
        grams,
        third_in,
    )

    weights_one = (second_in[:, None, :] * third_in[None, :, :]).astype(jnp.bfloat16)
    first_whole = lax.dot_general(
        tensor, weights_one, (((1, 2), (0, 1)), ((), ())), preferred_element_type=jnp.float32
    )
    first_whole = first_whole + jnp.dot(
        matrix, column_in.astype(jnp.bfloat16), preferred_element_type=jnp.float32
    )
    pieces, rows_first = pieces_of(first_whole, pair)
    raw_one, wide = solve_shared(sizes, ("ja", "ka"), 1, pieces, system.reshape(1, width, width))
    first_all = wide[:, :rows_first].reshape(total_first, width)
    first_gram = gram_of(first_all)
    scaling = lax.rsqrt(jnp.sum(first_all * first_all, axis=0) / total_first + 1e-06)
    gram_first = first_gram * scaling[:, None] * scaling[None, :]
    first_new = raw_one[:rows_first] * scaling
    first_mine = lax.dynamic_slice_in_dim(
        first_all, lax.axis_index("ia") * span_first, span_first, 0
    )
    first_half = (first_mine * scaling).astype(jnp.bfloat16)

    weights_two = (first_half.astype(jnp.float32)[:, None, :] * third_in[None, :, :]).astype(
        jnp.bfloat16
    )
    second_whole = lax.dot_general(
        tensor, weights_two, (((0, 2), (0, 1)), ((), ())), preferred_element_type=jnp.float32
    )
    column_whole = lax.dot_general(
        matrix, first_half, (((0,), (0,)), ((), ())), preferred_element_type=jnp.float32
    )
    systems = jnp.stack([gram_first * gram_third, gram_first])
    pieces, rows_second = pieces_of(second_whole, n_a * n_c)
    column_pieces, rows_column = pieces_of(column_whole, n_a)
    raw_two, wide, column_raw = solve_shared(
        sizes, ("ia", "ka"), 2, pieces, systems, column_pieces
    )
    second_all = wide[:, :rows_second].reshape(n_a, n_b, n_c, rows_second, width)
    second_all = second_all.transpose(1, 0, 2, 3, 4)
    second_mine = lax.dynamic_index_in_dim(second_all, lax.axis_index("ja"), 0, False)
    second_all = second_all.reshape(total_second, width)
    scaling = lax.rsqrt(jnp.sum(second_all * second_all, axis=0) / total_second + 1e-06)
    gram_updated = gram_of(second_all) * scaling[:, None] * scaling[None, :]
    second_new = raw_two[:rows_second] * scaling
    second_half = (second_mine.reshape(span_second, width) * scaling).astype(jnp.bfloat16)

    weights_three = (first_half[:, None, :] * second_half[None, :, :]).reshape(
        span_first * span_second, width
    )
    third_whole = lax.dot_general(
        tensor.reshape(span_first * span_second, span_third),
        weights_three,
        (((0,), (0,)), ((), ())),
        preferred_element_type=jnp.float32,
    )
    pieces, rows_third = pieces_of(third_whole, n_a * n_b)
    third_new, column_new = call(
        functools.partial(last_kernel, sizes, (total_third, total_column)),
        [shape(*pieces.shape[1:]), shape(*column_raw.shape)],
        [
            pltpu.VMEM(pieces.shape, jnp.float32),
            pltpu.VMEM((1, width, width), jnp.float32),
            pltpu.VMEM((8, width), jnp.float32),
            pltpu.VMEM((everyone, 8, width), jnp.float32),
            sems(pieces.shape[0]),
            sems(everyone),
        ],
        3,
        pieces,
        (gram_first * gram_updated)[None],
        column_raw,
    )
    return (first_new, second_new[None], third_new[:rows_third][None], column_new[:rows_column][None])


def solution(mesh):
    placed = (
        P("ia", "ja", "ka"),
        P("ia", ("ja", "ka")),
        P("ja", None),
        P("ka", None),
        P(("ja", "ka"), None),
    )
    return jax.shard_map(
        functools.partial(body, dict(mesh.shape)),
        mesh=mesh,
        in_specs=placed,
        out_specs=(
            P(("ia", "ja", "ka"), None),
            P("ja", ("ia", "ka"), None),
            P("ka", ("ia", "ja"), None),
            P(("ja", "ka"), "ia", None),
        ),
        check_vma=False,
    )
```

```python
import functools

import jax
import jax.numpy as jnp
from jax import lax
from jax.experimental import pallas as pl
from jax.experimental.pallas import tpu as pltpu
from jax.sharding import PartitionSpec as P

AXES = ("ia", "ja", "ka")
NEAR = ("ja", "ka")
FAR = ("ia",)
MESH = pl.DeviceIdType.MESH
HIGH = lax.Precision.HIGHEST
VMEM_LIMIT = 48 * 1024 * 1024


def dot_high(left, right, dims=(((1,), (0,)), ((), ()))):
    return lax.dot_general(
        left, right, dims, precision=HIGH, preferred_element_type=jnp.float32
    )


def gram_of(factor):
    return dot_high(factor, factor, (((0,), (0,)), ((), ())))


def group_size(sizes, axes):
    total = 1
    for axis in axes:
        total *= sizes[axis]
    return total


def place_in(sizes, axes):
    place = 0
    for axis in axes:
        place = place * sizes[axis] + lax.axis_index(axis)
    return place


def device_at(sizes, axes, place):
    coords = {}
    for axis in reversed(axes):
        coords[axis] = lax.rem(place, sizes[axis])
        place = place // sizes[axis]
    return tuple(coords[a] if a in coords else lax.axis_index(a) for a in AXES)


def enter(sizes, *groups):
    barrier = pltpu.get_barrier_semaphore()
    expected = 0
    for axes in groups:
        count = group_size(sizes, axes)
        me = place_in(sizes, axes)

        def greet(step, carry, axes=axes, count=count, me=me):
            peer = lax.rem(me + step, count)
            pl.semaphore_signal(
                barrier, inc=1, device_id=device_at(sizes, axes, peer), device_id_type=MESH
            )
            return carry

        lax.fori_loop(1, count, greet, 0)
        expected += count - 1
    pl.semaphore_wait(barrier, expected)


class Exchange:
    def __init__(self, sizes, axes, source, target, sems, at=()):
        self.sizes, self.axes = sizes, axes
        self.count = group_size(sizes, axes)
        self.me = place_in(sizes, axes)
        self.source, self.target, self.sems, self.at = source, target, sems, at

    def copy(self, step):
        peer = lax.rem(self.me + step, self.count)
        return pltpu.make_async_remote_copy(
            src_ref=self.source(peer),
            dst_ref=self.target(step, self.me),
            send_sem=self.sems.at[self.at + (0, step)],
            recv_sem=self.sems.at[self.at + (1, step)],
            device_id=device_at(self.sizes, self.axes, peer),
            device_id_type=MESH,
        )

    def start(self):
        def one(step, carry):
            self.copy(step).start()
            return carry

        lax.fori_loop(1, self.count, one, 0)

    def wait(self):
        def one(step, carry):
            self.copy(step).wait()
            return carry

        lax.fori_loop(1, self.count, one, 0)


def add_slots(first, slots, count):
    return lax.fori_loop(1, count, lambda step, total: total + slots[step], first)


def sweep(d, k, few, lane, line, cross):
    top = lane[:1]
    small, below, scale, rows, cols = {}, {}, [], [], []
    for i in range(few):
        at = k + i
        rows.append(
            jnp.where((top >= k) & (top < k + few), jnp.where(top == at, -1.0, 0.0), d[at : at + 1, :])
        )
        side = line[:, :1]
        cols.append(
            jnp.where(
                (side >= k) & (side < k + few), jnp.where(side == at, -1.0, 0.0), d[:, at : at + 1]
            )
        )
        for j in range(i, few):
            small[i, j] = jnp.broadcast_to(d[at : at + 1, k + j : k + j + 1], top.shape)
    for p in range(few):
        scale.append(1.0 / small[p, p])
        for i in range(p + 1, few):
            below[i, p] = small[p, i] * scale[p]
            for j in range(i, few):
                small[i, j] = small[i, j] - below[i, p] * small[p, j]
    for i in range(few):
        for p in range(i):
            rows[i] = rows[i] - below[i, p] * rows[p]
    solved = [rows[i] * scale[i] for i in range(few)]
    for i in reversed(range(few)):
        for p in range(i + 1, few):
            solved[i] = solved[i] - below[p, i] * solved[p]
    total = jnp.where(cross, 0.0, d)
    for i in range(few):
        total = total - cols[i] * solved[i]
    return total


class Gather:
    def __init__(self, sizes, stage, wide, near_sems, far_sems):
        self.sizes, self.wide, self.far_sems = sizes, wide, far_sems
        self.pair = group_size(sizes, NEAR)
        self.base = lax.axis_index("ia") * self.pair
        self.me = place_in(sizes, NEAR)
        base = self.base
        self.near = Exchange(
            sizes, NEAR, lambda p: stage, lambda s, me: wide.at[base + me], near_sems
        )

    def far(self, step):
        block = self.base + lax.rem(self.me - step + self.pair, self.pair)
        return Exchange(
            self.sizes,
            FAR,
            lambda p: self.wide.at[block],
            lambda s, me: self.wide.at[block],
            self.far_sems,
            (step,),
        )

    def start(self, mine):
        self.wide[self.base + self.me] = mine
        self.near.start()
        self.far(0).start()

        def one(step, carry):
            self.near.copy(step).wait()
            self.far(step).start()
            return carry

        lax.fori_loop(1, self.pair, one, 0)

    def wait(self):
        def one(step, carry):
            self.far(step).wait()
            return carry

        lax.fori_loop(0, self.pair, one, 0)


def invert(block, few, a_ref, out_ref):
    many, width, _ = a_ref.shape
    out_ref[...] = a_ref[...]
    lane = lax.broadcasted_iota(jnp.int32, (block, block), 1)
    line = lax.broadcasted_iota(jnp.int32, (block, block), 0)
    wide_lane = lax.broadcasted_iota(jnp.int32, (block, width), 1)
    wide_line = lax.broadcasted_iota(jnp.int32, (block, width), 0)
    for start in range(0, width, block):
        stop = start + block
        rows = [out_ref[m, start:stop, :] for m in range(many)]
        pivots = [r[:, start:stop] for r in rows]
        for k in range(0, block, few):
            cross = ((lane >= k) & (lane < k + few)) | ((line >= k) & (line < k + few))
            for m in range(many):
                pivots[m] = sweep(pivots[m], k, few, lane, line, cross)
        own = (wide_lane >= start) & (wide_lane < stop)
        picked = jnp.where(wide_lane == wide_line + start, -1.0, 0.0)
        for m in range(many):
            sides = jnp.where(own, picked, rows[m])
            scaled = dot_high(pivots[m], sides)
            update = dot_high(sides, scaled, (((0,), (0,)), ((), ())))
            whole = out_ref[m]
            at_line = lax.broadcasted_iota(jnp.int32, whole.shape, 0)
            at_lane = lax.broadcasted_iota(jnp.int32, whole.shape, 1)
            gone = ((at_line >= start) & (at_line < stop)) | (
                (at_lane >= start) & (at_lane < stop)
            )
            out_ref[m] = jnp.where(gone, 0.0, whole) + update
    out_ref[...] = -out_ref[...]


def block_of(width):
    return 64 if width % 64 == 0 else 8


def call(kernel, outs, scratch, ident, *operands):
    return pl.pallas_call(
        kernel,
        out_shape=outs,
        in_specs=[pl.BlockSpec(memory_space=pltpu.VMEM)] * len(operands),
        out_specs=[pl.BlockSpec(memory_space=pltpu.VMEM)] * len(outs),
        scratch_shapes=scratch,
        compiler_params=pltpu.CompilerParams(
            collective_id=ident, has_side_effects=True, vmem_limit_bytes=VMEM_LIMIT
        ),
    )(*operands)


def sems(count):
    return pltpu.SemaphoreType.DMA((2, count))


def shape(*dims, dtype=jnp.float32):
    return jax.ShapeDtypeStruct(dims, dtype)


def system_kernel(sizes, grams, third, system, gram_third, got, thirds, stage, s0, s1, s2):
    group = ("ja", "ka")
    count, rows = grams.shape[0], grams.shape[1] // 2
    enter(sizes, group)
    spread = Exchange(sizes, group, lambda p: grams.at[p], lambda s, me: got.at[s], s0)
    share = Exchange(sizes, ("ka",), lambda p: third, lambda s, me: thirds.at[s], s1)
    spread.start()
    share.start()
    total = gram_of(third[...])
    share.wait()
    for step in range(1, sizes["ka"]):
        total = total + gram_of(thirds[step])
    gram_third[...] = total
    spread.wait()
    me = spread.me
    summed = add_slots(grams[me], got, count)
    mine = summed[:rows] * gram_third[pl.ds(pl.multiple_of(me * rows, 8), rows), :]
    mine = mine + summed[rows:]
    stage[...] = mine
    system[me] = mine
    spread_back = Exchange(sizes, group, lambda p: stage, lambda s, me: system.at[me], s2)
    spread_back.start()
    spread_back.wait()


def solve_kernel(sizes, group, with_column, *refs):
    if with_column:
        pieces, systems, column, mine, wide, column_raw, got, inverse, stage, s0, s1, far = refs[:12]
        got_column, s2 = refs[12:]
    else:
        pieces, systems, mine, wide, got, inverse, stage, s0, s1, far = refs
    enter(sizes, NEAR, group if with_column else FAR)
    spread = Exchange(sizes, group, lambda p: pieces.at[p], lambda s, me: got.at[s], s0)
    spread.start()
    if with_column:
        side = Exchange(
            sizes, ("ia",), lambda p: column.at[p], lambda s, me: got_column.at[s], s2
        )
        side.start()
    invert(block_of(systems.shape[-1]), 4, systems, inverse)
    spread.wait()
    raw = dot_high(add_slots(pieces[spread.me], got, spread.count), inverse[0])
    mine[...] = raw
    stage[...] = raw
    back = Gather(sizes, stage, wide, s1, far)
    back.start(raw)
    if with_column:
        side.wait()
        total = add_slots(column[side.me], got_column, side.count)
        column_raw[...] = dot_high(total, inverse[1])
    back.wait()


def solve_shared(sizes, group, ident, pieces, systems, column=None):
    count, rows, width = pieces.shape
    everyone = group_size(sizes, AXES)
    outs = [shape(rows, width), shape(everyone, rows, width)]
    scratch = [
        pltpu.VMEM(pieces.shape, jnp.float32),
        pltpu.VMEM(systems.shape, jnp.float32),
        pltpu.VMEM((rows, width), jnp.float32),
        sems(count),
        sems(group_size(sizes, NEAR)),
        pltpu.SemaphoreType.DMA((group_size(sizes, NEAR), 2, sizes["ia"])),
    ]
    operands = [pieces, systems]
    if column is not None:
        outs.append(shape(*column.shape[1:]))
        operands.append(column)
        scratch += [pltpu.VMEM(column.shape, column.dtype), sems(column.shape[0])]
    kernel = functools.partial(solve_kernel, sizes, group, column is not None)
    return call(kernel, outs, scratch, ident, *operands)


def last_kernel(
    sizes, totals, pieces, systems, column, third, column_out, got, inverse, stage, sums, stage_far, sums_far, s0, s1, s2
):
    group = ("ia", "ja")
    enter(sizes, group, NEAR)
    spread = Exchange(sizes, group, lambda p: pieces.at[p], lambda s, me: got.at[s], s0)
    spread.start()
    invert(block_of(systems.shape[-1]), 4, systems, inverse)
    column_raw = column[...]
    column_square = jnp.sum(column_raw * column_raw, axis=0, keepdims=True)
    spread.wait()
    raw = dot_high(add_slots(pieces[spread.me], got, spread.count), inverse[0])
    square = jnp.sum(raw * raw, axis=0, keepdims=True)
    line = lax.broadcasted_iota(jnp.int32, stage.shape, 0)
    mine = jnp.where(line == 0, square, jnp.where(line == 1, column_square, 0.0))
    stage[...] = mine
    back = Exchange(sizes, NEAR, lambda p: stage, lambda s, me: sums.at[s], s1)
    back.start()
    back.wait()
    mine = add_slots(mine, sums, back.count)
    stage_far[...] = mine
    last = Exchange(sizes, FAR, lambda p: stage_far, lambda s, me: sums_far.at[s], s2)
    last.start()
    last.wait()
    whole = add_slots(mine, sums_far, last.count)
    third[...] = raw * lax.rsqrt(whole[0:1] / totals[0] + 1e-06)
    column_out[...] = column_raw * lax.rsqrt(whole[1:2] / totals[1] + 1e-06)


def pieces_of(whole, count):
    rows = whole.shape[0] // count
    pieces = whole.reshape(count, rows, whole.shape[1])
    return jnp.pad(pieces, ((0, 0), (0, -rows % 8), (0, 0))), rows


def body(sizes, tensor, matrix, second_in, third_in, column_in):
    n_a, n_b, n_c = (sizes[a] for a in AXES)
    span_first, span_second, span_third = tensor.shape
    width = second_in.shape[1]
    total_first, total_second = span_first * n_a, span_second * n_b
    total_third, total_column = span_third * n_c, matrix.shape[1] * n_b * n_c

    pair = n_b * n_c
    grams = jnp.concatenate(
        [
            (gram_of(second_in) * (1.0 / n_c)).reshape(pair, width // pair, width),
            gram_of(column_in).reshape(pair, width // pair, width),
        ],
        axis=1,
    )
    rows = width // pair
    system, gram_third = call(
        functools.partial(system_kernel, sizes),
        [shape(pair, rows, width), shape(width, width)],
        [
            pltpu.VMEM(grams.shape, jnp.float32),
            pltpu.VMEM((n_c,) + third_in.shape, jnp.float32),
            pltpu.VMEM((rows, width), jnp.float32),
            sems(pair),
            sems(n_c),
            sems(pair),
        ],
        0,
        grams,
        third_in,
    )

    weights_one = (second_in[:, None, :] * third_in[None, :, :]).astype(jnp.bfloat16)
    first_whole = lax.dot_general(
        tensor, weights_one, (((1, 2), (0, 1)), ((), ())), preferred_element_type=jnp.float32
    )
    first_whole = first_whole + jnp.dot(
        matrix, column_in.astype(jnp.bfloat16), preferred_element_type=jnp.float32
    )
    pieces, rows_first = pieces_of(first_whole, pair)
    raw_one, wide = solve_shared(sizes, ("ja", "ka"), 1, pieces, system.reshape(1, width, width))
    first_all = wide[:, :rows_first].reshape(total_first, width)
    first_gram = gram_of(first_all)
    scaling = lax.rsqrt(jnp.sum(first_all * first_all, axis=0) / total_first + 1e-06)
    gram_first = first_gram * scaling[:, None] * scaling[None, :]
    first_new = raw_one[:rows_first] * scaling
    first_mine = lax.dynamic_slice_in_dim(
        first_all, lax.axis_index("ia") * span_first, span_first, 0
    )
    first_half = (first_mine * scaling).astype(jnp.bfloat16)

    weights_two = (first_half.astype(jnp.float32)[:, None, :] * third_in[None, :, :]).astype(
        jnp.bfloat16
    )
    second_whole = lax.dot_general(
        tensor, weights_two, (((0, 2), (0, 1)), ((), ())), preferred_element_type=jnp.float32
    )
    column_whole = lax.dot_general(
        matrix, first_half, (((0,), (0,)), ((), ())), preferred_element_type=jnp.float32
    )
    systems = jnp.stack([gram_first * gram_third, gram_first])
    pieces, rows_second = pieces_of(second_whole, n_a * n_c)
    column_pieces, rows_column = pieces_of(column_whole, n_a)
    raw_two, wide, column_raw = solve_shared(
        sizes, ("ia", "ka"), 2, pieces, systems, column_pieces
    )
    second_all = wide[:, :rows_second].reshape(n_a, n_b, n_c, rows_second, width)
    second_all = second_all.transpose(1, 0, 2, 3, 4)
    second_mine = lax.dynamic_index_in_dim(second_all, lax.axis_index("ja"), 0, False)
    second_all = second_all.reshape(total_second, width)
    scaling = lax.rsqrt(jnp.sum(second_all * second_all, axis=0) / total_second + 1e-06)
    gram_updated = gram_of(second_all) * scaling[:, None] * scaling[None, :]
    second_new = raw_two[:rows_second] * scaling
    second_half = (second_mine.reshape(span_second, width) * scaling).astype(jnp.bfloat16)

    weights_three = (first_half[:, None, :] * second_half[None, :, :]).reshape(
        span_first * span_second, width
    )
    third_whole = lax.dot_general(
        tensor.reshape(span_first * span_second, span_third),
        weights_three,
        (((0,), (0,)), ((), ())),
        preferred_element_type=jnp.float32,
    )
    pieces, rows_third = pieces_of(third_whole, n_a * n_b)
    third_new, column_new = call(
        functools.partial(last_kernel, sizes, (total_third, total_column)),
        [shape(*pieces.shape[1:]), shape(*column_raw.shape)],
        [
            pltpu.VMEM(pieces.shape, jnp.float32),
            pltpu.VMEM((1, width, width), jnp.float32),
            pltpu.VMEM((8, width), jnp.float32),
            pltpu.VMEM((pair, 8, width), jnp.float32),
            pltpu.VMEM((8, width), jnp.float32),
            pltpu.VMEM((n_a, 8, width), jnp.float32),
            sems(pieces.shape[0]),
            sems(pair),
            sems(n_a),
        ],
        3,
        pieces,
        (gram_first * gram_updated)[None],
        column_raw,
    )
    return (first_new, second_new[None], third_new[:rows_third][None], column_new[:rows_column][None])


def solution(mesh):
    placed = (
        P("ia", "ja", "ka"),
        P("ia", ("ja", "ka")),
        P("ja", None),
        P("ka", None),
        P(("ja", "ka"), None),
    )
    return jax.shard_map(
        functools.partial(body, dict(mesh.shape)),
        mesh=mesh,
        in_specs=placed,
        out_specs=(
            P(("ia", "ja", "ka"), None),
            P("ja", ("ia", "ka"), None),
            P("ka", ("ia", "ja"), None),
            P(("ja", "ka"), "ia", None),
        ),
        check_vma=False,
    )
```
